256 devices in a mesh: adapter: 16 (over x_lo, y, core), tensor: 16 (over x_hi, z).
Axes of the slice: x: 4 (x_hi: 2, x_lo: 2; x = x_hi * 2 + x_lo), y: 4, z: 8, core: 2. Of those that a mesh axis runs over, the one named last changes fastest.
Arguments:
- tokens: bfloat16 [8192, 8192], P('adapter', 'tensor'), may hold values from -6 to 6
- cotangent: bfloat16 [8192, 8192], P('adapter', 'tensor'), may hold values from -1.5 to 1.5
- frozen_weight: bfloat16 [8192, 8192], P('adapter', 'tensor'), may hold values from -0.0625 to 0.0625
- adapter_per_tile: int32 [16, 4], P('adapter'), may hold values from 0 to 63, as said below
- tile_token_length: int32 [16, 4], P('adapter'), may hold values from 1 to 128, as said below
- adapter_down_weight: float32 [64, 64, 8192], P('adapter', None, 'tensor'), may hold values from -0.0625 to 0.0625
- adapter_up_weight: float32 [64, 64, 8192], P('adapter', None, 'tensor'), may hold values from -0.1875 to 0.1875
- down_first_moment: float32 [64, 64, 8192], P('adapter', None, 'tensor'), may hold values from -18 to 18
- down_second_moment: float32 [64, 64, 8192], P('adapter', None, 'tensor'), may hold values from 0.03 to 0.3
- up_first_moment: float32 [64, 64, 8192], P('adapter', None, 'tensor'), may hold values from -6 to 6
- up_second_moment: float32 [64, 64, 8192], P('adapter', None, 'tensor'), may hold values from 0.003 to 0.03
Outputs:
- output: bfloat16 [8192, 8192], P('adapter', 'tensor')
- token_gradient: bfloat16 [8192, 8192], P('adapter', 'tensor')
- fresh_down_weight: float32 [64, 64, 8192], P('adapter', None, 'tensor')
- fresh_up_weight: float32 [64, 64, 8192], P('adapter', None, 'tensor')
- fresh_down_first_moment: float32 [64, 64, 8192], P('adapter', None, 'tensor')
- fresh_down_second_moment: float32 [64, 64, 8192], P('adapter', None, 'tensor')
- fresh_up_first_moment: float32 [64, 64, 8192], P('adapter', None, 'tensor')
- fresh_up_second_moment: float32 [64, 64, 8192], P('adapter', None, 'tensor')
The draws below stay inside these ranges and needn't reach their ends.
Inputs may be any that keep to these rules, and one draw needn't show every extreme that they name: `adapter_per_tile`: adapter k * 4 + j belongs to owner k. The 4 tiles of one batch shard belong to adapters of 4 different owners; in every draw some owner has a tile from every batch shard. `tile_token_length`: the first tile of every batch shard is full.
All inputs are finite; a program needn't handle non-finite values.
Results may differ from the reference program's by a relative error of at most 0.02.
Values may be sent and summed in bfloat16 or wider, within the bound.
No kernel may reach another device: no remote copies, remote signals or barrier semaphores. Data moves between devices by JAX's collectives and lax.ppermute only.
A program may use at most 128 MiB of HBM per device.

```python
import math
import jax
import jax.numpy as jnp
from jax import lax

MODEL_WIDTH = 8192
ADAPTER_RANK = 64
ADP_DEV = 4
TILE = 128
TOK_DEV = 512
ADAM_STEP = 10
ADAPTER_TOTAL = 64
TOKEN_ROWS = 8192
N_TENSOR = 16


def draw_adapter_per_tile(key, part):
    key = jax.random.fold_in(key, 11)
    owners = ADAPTER_TOTAL // ADP_DEV
    tile_count = TOK_DEV // TILE
    hot_key, rest_key = jax.random.split(key)
    hot_owner = jax.random.randint(hot_key, (), 0, owners, dtype=jnp.int32)
    device_keys = jax.random.split(rest_key, owners)

    def per_device(device_key):
        perm_key, order_key, within_key = jax.random.split(device_key, 3)
        others = jax.random.permutation(perm_key, owners - 1).astype(jnp.int32)
        others = others + (others >= hot_owner).astype(jnp.int32)
        chosen = jnp.concatenate([hot_owner[None], others[:tile_count - 1]])
        chosen = jax.random.permutation(order_key, chosen)
        within = jax.random.randint(within_key, (tile_count,), 0, ADP_DEV, dtype=jnp.int32)
        return chosen * ADP_DEV + within
    return jax.vmap(per_device)(device_keys).astype(jnp.int32)


def draw_tile_token_length(key, part):
    key = jax.random.fold_in(key, 12)
    owners = ADAPTER_TOTAL // ADP_DEV
    tile_count = TOK_DEV // TILE
    drawn = jax.random.randint(key, (owners, tile_count), 1, TILE + 1, dtype=jnp.int32)
    column = jnp.arange(tile_count, dtype=jnp.int32)[None, :]
    return jnp.where(column == 0, TILE, drawn).astype(jnp.int32)


def shard_levels(stream_key, extent, cuts, least, top_value):
    def one(axis_at, blocks):
        steps = jax.random.uniform(jax.random.fold_in(jax.random.fold_in(stream_key, 6), axis_at), (blocks,), jnp.float32, least / len(cuts), top_value / len(cuts))
        return jnp.repeat(jnp.exp(steps), extent[axis_at] // blocks).reshape((-1,) + (1,) * (len(extent) - axis_at - 1))

    factor_of = one(*cuts[0])
    for cut in cuts[1:]:
        factor_of = factor_of * one(*cut)
    return factor_of


def normal_values(stream_key, shape, spread, most, cuts=(), held_as=jnp.bfloat16):
    array = spread * jax.random.normal(stream_key, shape, jnp.float32)
    if cuts:
        array = array * shard_levels(stream_key, shape, cuts, -0.22, 0.18)
    return jnp.clip(array, -most, most).astype(held_as)


def setup_inputs(seed: int = 0) -> dict:
    key_list = jax.random.split(jax.random.key(seed), 12)
    tokens = normal_values(key_list[0], (TOKEN_ROWS, MODEL_WIDTH), 1.0, 6.0, ((0, 16), (1, 16)))
    cotangent = normal_values(key_list[1], (TOKEN_ROWS, MODEL_WIDTH), 0.25, 1.5, ((0, 16), (1, 16)))
    frozen_weight = normal_values(key_list[2], (MODEL_WIDTH, MODEL_WIDTH), MODEL_WIDTH ** -0.5, 0.0625, ((0, 16), (1, 16)))
    adapter_per_tile = draw_adapter_per_tile(jax.random.fold_in(key_list[11], 71), 0)
    tile_token_length = draw_tile_token_length(jax.random.fold_in(key_list[11], 71), 0)
    adapter_down_weight = normal_values(key_list[5], (ADAPTER_TOTAL, ADAPTER_RANK, MODEL_WIDTH), MODEL_WIDTH ** -0.5, 0.0625, ((0, 16), (2, 16)), jnp.float32)
    adapter_up_weight = normal_values(key_list[6], (ADAPTER_TOTAL, ADAPTER_RANK, MODEL_WIDTH), (MODEL_WIDTH // 8) ** -0.5, 0.1875, ((0, 16), (2, 16)), jnp.float32)
    down_first_moment = normal_values(key_list[7], (ADAPTER_TOTAL, ADAPTER_RANK, MODEL_WIDTH), 3.0, 18.0, ((0, 16), (2, 16)), jnp.float32)
    down_second_moment = jnp.clip(jnp.exp(math.log(0.3) - 2.3025852 * jax.random.uniform(key_list[8], (ADAPTER_TOTAL, ADAPTER_RANK, MODEL_WIDTH), jnp.float32) ** shard_levels(key_list[8], (ADAPTER_TOTAL, ADAPTER_RANK, MODEL_WIDTH), ((0, 16), (2, 16)), -0.2, 0.2)), 0.03, 0.3)
    up_first_moment = normal_values(key_list[9], (ADAPTER_TOTAL, ADAPTER_RANK, MODEL_WIDTH), 1.0, 6.0, ((0, 16), (2, 16)), jnp.float32)
    up_second_moment = jnp.clip(jnp.exp(math.log(0.03) - 2.3025851 * jax.random.uniform(key_list[10], (ADAPTER_TOTAL, ADAPTER_RANK, MODEL_WIDTH), jnp.float32) ** shard_levels(key_list[10], (ADAPTER_TOTAL, ADAPTER_RANK, MODEL_WIDTH), ((0, 16), (2, 16)), -0.2, 0.2)), 0.003, 0.03)
    return dict(tokens=tokens, cotangent=cotangent, frozen_weight=frozen_weight, adapter_per_tile=adapter_per_tile, tile_token_length=tile_token_length, adapter_down_weight=adapter_down_weight, adapter_up_weight=adapter_up_weight, down_first_moment=down_first_moment, down_second_moment=down_second_moment, up_first_moment=up_first_moment, up_second_moment=up_second_moment)


adapter_scale = 0.5
beta_one = 0.9
beta_two = 0.999
adam_eps = 1e-08
weight_decay = 0.01
learn_rate = 0.001

def decoupled_adam(parameter, moment, second, gradient):
    moment_new = beta_one * moment + (1.0 - beta_one) * gradient
    second_new = beta_two * second + (1.0 - beta_two) * gradient * gradient
    bias_first = 1.0 - beta_one ** ADAM_STEP
    bias_second = 1.0 - beta_two ** ADAM_STEP
    update = moment_new / bias_first / (jnp.sqrt(second_new / bias_second) + adam_eps) + weight_decay * parameter
    return (parameter - learn_rate * update, moment_new, second_new)

def reference(tokens, cotangent, frozen_weight, adapter_per_tile, tile_token_length, adapter_down_weight, adapter_up_weight, down_first_moment, down_second_moment, up_first_moment, up_second_moment):
    tile_adapter_index = adapter_per_tile.reshape(-1).astype(jnp.int32)
    tile_len = tile_token_length.reshape(-1).astype(jnp.int32)
    tile_count = tile_adapter_index.shape[0]
    position = jnp.arange(TILE, dtype=jnp.int32)
    kept_rows = position[None, :] < tile_len[:, None]
    x_tiles = tokens.reshape(tile_count, TILE, MODEL_WIDTH)
    dy_tiles = jnp.where(kept_rows[:, :, None], cotangent.reshape(tile_count, TILE, MODEL_WIDTH), jnp.zeros((), jnp.bfloat16))
    down_tile_rows = adapter_down_weight.astype(jnp.bfloat16)[tile_adapter_index].astype(jnp.float32)
    up_tile_rows = adapter_up_weight.astype(jnp.bfloat16)[tile_adapter_index].astype(jnp.float32)
    input_full = x_tiles.astype(jnp.float32)
    output_gradient_full = dy_tiles.astype(jnp.float32)
    narrow_forward_pass = jnp.einsum('nkf,nrf->nkr', input_full, down_tile_rows).astype(jnp.bfloat16)
    adapter_output = (adapter_scale * jnp.einsum('uys,usl->uyl', narrow_forward_pass.astype(jnp.float32), up_tile_rows)).astype(jnp.bfloat16)
    frozen_output = jnp.dot(tokens, frozen_weight, preferred_element_type=jnp.float32)
    output = (frozen_output + adapter_output.reshape(TOKEN_ROWS, MODEL_WIDTH).astype(jnp.float32)).astype(jnp.bfloat16)
    narrow_backward_pass = jnp.einsum('nkf,nrf->nkr', output_gradient_full, up_tile_rows).astype(jnp.bfloat16)
    adapter_gradient = (adapter_scale * jnp.einsum('uys,usl->uyl', narrow_backward_pass.astype(jnp.float32), down_tile_rows)).astype(jnp.bfloat16)
    dy_flat = dy_tiles.reshape(TOKEN_ROWS, MODEL_WIDTH)
    block_width = MODEL_WIDTH // N_TENSOR

    def add_block(block_index, running):
        offset = (block_index * block_width).astype(jnp.int32)
        columns = lax.dynamic_slice_in_dim(dy_flat, offset, block_width, 1)
        weights = lax.dynamic_slice_in_dim(frozen_weight, offset, block_width, 1)
        partial_sum = lax.dot_general(columns, weights, (((1,), (1,)), ((), ())), preferred_element_type=jnp.float32)
        rounded = lax.optimization_barrier(partial_sum.astype(jnp.bfloat16))
        return running + rounded.astype(jnp.float32)
    reduced_total = lax.fori_loop(0, N_TENSOR, add_block, jnp.zeros((TOKEN_ROWS, MODEL_WIDTH), jnp.float32))
    token_gradient = (reduced_total + adapter_gradient.reshape(TOKEN_ROWS, MODEL_WIDTH).astype(jnp.float32)).astype(jnp.bfloat16)
    indicator_matrix = (tile_adapter_index[:, None] == jnp.arange(ADAPTER_TOTAL, dtype=jnp.int32)[None, :]).astype(jnp.float32)
    local_up_weight = adapter_scale * jnp.einsum('ajc,ajm->acm', narrow_forward_pass.astype(jnp.float32), output_gradient_full)
    up_gradient = jnp.einsum('np,nrf->prf', indicator_matrix, local_up_weight, precision=lax.Precision.HIGHEST)
    local_down_weight = adapter_scale * jnp.einsum('ajc,ajm->acm', narrow_backward_pass.astype(jnp.float32), input_full)
    down_gradient = jnp.einsum('np,nrf->prf', indicator_matrix, local_down_weight, precision=lax.Precision.HIGHEST)
    fresh_down_weight, fresh_down_first_moment, fresh_down_second_moment = decoupled_adam(adapter_down_weight, down_first_moment, down_second_moment, down_gradient)
    fresh_up_weight, fresh_up_first_moment, fresh_up_second_moment = decoupled_adam(adapter_up_weight, up_first_moment, up_second_moment, up_gradient)
    return (output, token_gradient, fresh_down_weight, fresh_up_weight, fresh_down_first_moment, fresh_down_second_moment, fresh_up_first_moment, fresh_up_second_moment)
```

```python
import functools

import jax
import jax.numpy as jnp
from jax import lax
from jax.experimental import pallas as pl
from jax.experimental.pallas import tpu as pltpu
from jax.sharding import Mesh
from jax.sharding import PartitionSpec as P

ADAM_STEP = 10

adapter_scale = 0.5
beta_one = 0.9
beta_two = 0.999
adam_eps = 1e-08
weight_decay = 0.01
learn_rate = 0.001

VMEM = pl.BlockSpec(memory_space=pltpu.VMEM)
SMEM = pl.BlockSpec(memory_space=pltpu.SMEM)
ADAPTER = ("xl", "y", "c")
TENSOR = ("xh", "z")
NT = (((1,), (1,)), ((), ()))
TN = (((0,), (0,)), ((), ()))
NN = (((1,), (0,)), ((), ()))


def dot(a, b, dims):
    return lax.dot_general(a, b, dims, preferred_element_type=jnp.float32)


def call(kernel, out_shape, args, scalars, flops, moved, limit=40, scratch=()):
    return pl.pallas_call(
        kernel,
        out_shape=out_shape,
        in_specs=[SMEM] * len(scalars) + [VMEM] * len(args),
        out_specs=jax.tree.map(lambda _: VMEM, out_shape),
        scratch_shapes=list(scratch),
        compiler_params=pltpu.CompilerParams(vmem_limit_bytes=limit * 2**20),
        cost_estimate=pl.CostEstimate(flops=flops, bytes_accessed=moved, transcendentals=0),
    )(*scalars, *args)


def decoupled_adam(parameter, moment, second, gradient):
    moment_new = beta_one * moment + (1.0 - beta_one) * gradient
    second_new = beta_two * second + (1.0 - beta_two) * gradient * gradient
    bias_first = 1.0 - beta_one**ADAM_STEP
    bias_second = 1.0 - beta_two**ADAM_STEP
    update = (
        moment_new / bias_first / (jnp.sqrt(second_new / bias_second) + adam_eps)
        + weight_decay * parameter
    )
    return (parameter - learn_rate * update, moment_new, second_new)


def select_kernel(slot_ref, down_ref, up_ref, send_ref, both_ref):
    rank = down_ref.shape[1]
    both_ref[:, :rank] = down_ref[...].astype(jnp.bfloat16)
    both_ref[:, rank:] = up_ref[...].astype(jnp.bfloat16)
    held = down_ref.shape[0]

    @pl.loop(0, send_ref.shape[0])
    def _(peer):
        send_ref[peer] = both_ref[jnp.minimum(slot_ref[peer], held - 1)]


def low_kernel(owner_ref, x_ref, dy_ref, weight_ref, low_ref):
    tiles = owner_ref.shape[0]
    height = x_ref.shape[0] // tiles
    rank = weight_ref.shape[1] // 2
    for j in range(tiles):
        rows = pl.ds(j * height, height)
        weight = weight_ref[owner_ref[j]]
        fwd = dot(x_ref[rows], weight, NT)
        bwd = dot(dy_ref[rows], weight, NT)
        lane = lax.broadcasted_iota(jnp.int32, fwd.shape, 1)
        low_ref[rows] = jnp.where(lane < rank, fwd, bwd).astype(jnp.bfloat16)


def grad_kernel(owner_ref, low_ref, x_ref, dy_ref, weight_ref, send_ref, out_ref, back_ref):
    tiles = owner_ref.shape[0]
    height = x_ref.shape[0] // tiles
    rank = weight_ref.shape[1] // 2
    send_ref[...] = jnp.zeros_like(send_ref)
    for j in range(tiles):
        rows = pl.ds(j * height, height)
        owner = owner_ref[j]
        weight = weight_ref[owner]
        low = low_ref[rows]
        fwd, bwd = low[:, :rank], low[:, rank:]
        out_ref[rows] = (adapter_scale * dot(fwd, weight[rank:], NN)).astype(jnp.bfloat16)
        back_ref[rows] = (adapter_scale * dot(bwd, weight[:rank], NN)).astype(jnp.bfloat16)
        up_part = dot(low, dy_ref[rows], TN)[:rank]
        down_part = dot(low, x_ref[rows], TN)[rank:]
        part = jnp.concatenate([down_part, up_part], axis=0)
        send_ref[owner] = (adapter_scale * part).astype(jnp.bfloat16)


def adam_kernel(slot_ref, part_ref, pd, pu, md, vd, mu, vu, npd, npu, nmd, nvd, nmu, nvu, acc):
    held, rank, _ = pd.shape
    acc[...] = jnp.zeros_like(acc)

    @pl.loop(0, part_ref.shape[0])
    def _(peer):
        slot = slot_ref[peer]

        @pl.when(slot < held)
        def _():
            acc[slot] += part_ref[peer].astype(jnp.float32)

    for k in range(held):
        npd[k], nmd[k], nvd[k] = decoupled_adam(pd[k], md[k], vd[k], acc[k, :rank])
        npu[k], nmu[k], nvu[k] = decoupled_adam(pu[k], mu[k], vu[k], acc[k, rank:])


def back_kernel(at_ref, mine_ref, theirs_ref, *refs):
    weights, out_ref = refs[:-1], refs[-1]
    xh = at_ref[0]
    for i, weight in enumerate(weights):
        total = dot(mine_ref[...], weight[xh], NT) + dot(theirs_ref[...], weight[1 - xh], NT)
        out_ref[at_ref[1 + i]] = total.astype(jnp.bfloat16)


def forward_kernel(at_ref, x_ref, *refs, theirs):
    weights, out_ref = refs[:-1], refs[-1]
    column = 1 - at_ref[0] if theirs else at_ref[0]
    total = dot(x_ref[at_ref[1]], weights[0][column], NN)
    for i, weight in enumerate(weights[1:], 1):
        total += dot(x_ref[at_ref[1 + i]], weight[column], NN)
    out_ref[...] = total.astype(out_ref.dtype)


def per_device(
    tokens,
    cotangent,
    frozen_weight,
    adapter_per_tile,
    tile_token_length,
    adapter_down_weight,
    adapter_up_weight,
    down_first_moment,
    down_second_moment,
    up_first_moment,
    up_second_moment,
):
    bf16, f32 = jnp.bfloat16, jnp.float32
    tok_rows, width = tokens.shape
    tile_count = adapter_per_tile.shape[1]
    tile_rows = tok_rows // tile_count
    held, rank, _ = adapter_down_weight.shape
    owners = lax.axis_size(ADAPTER)
    peers = lax.axis_size(TENSOR)
    planes = lax.axis_size("z")
    ys = lax.axis_size("y")
    xl, y, c, xh = (lax.axis_index(n) for n in ("xl", "y", "c", "xh"))

    adapters_here = adapter_per_tile[0]
    owner_of = adapters_here // held
    chosen = owner_of[None, :] == jnp.arange(owners, dtype=jnp.int32)[:, None]
    asked = jnp.sum(jnp.where(chosen, adapters_here[None, :] % held - held, 0), axis=1) + held
    slots = lax.all_to_all(
        asked.reshape(owners, 1, 1), ADAPTER, split_axis=0, concat_axis=0, tiled=True
    ).reshape(owners)

    swap = [(0, 1), (1, 0)]
    position = jnp.arange(tile_rows, dtype=jnp.int32)
    kept = position[None, :] < tile_token_length[0][:, None]
    dy = jnp.where(
        kept[:, :, None],
        cotangent.reshape(tile_count, tile_rows, width),
        jnp.zeros((), bf16),
    ).reshape(tok_rows, width)
    dy_theirs = lax.ppermute(dy, "xh", swap)

    x_all = lax.all_gather(tokens, "z", axis=0)

    sites = [(0, 0), (1, 0), (0, 1), (1, 1)]
    place = [a * 2 + b for a, b in sites]
    first = lax.ppermute(
        frozen_weight, ("xl", "xh"), [(place[0], place[1]), (place[1], place[2]), (place[2], place[0])]
    )
    second = lax.ppermute(
        frozen_weight, ("xl", "xh"), [(place[1], place[3]), (place[2], place[1]), (place[3], place[2])]
    )
    x_site = xh * 2 + xl
    block_a = jnp.where(x_site == 0, frozen_weight, jnp.where(x_site == 3, second, first))
    block_b = jnp.where(x_site == 3, frozen_weight, jnp.where(x_site == 0, first, second))
    here = jnp.stack([block_a, block_b])

    sent = call(
        select_kernel,
        jax.ShapeDtypeStruct((owners, 2 * rank, width), bf16),
        [adapter_down_weight, adapter_up_weight],
        [slots],
        0,
        3 * 2**20,
        scratch=[pltpu.VMEM((held, 2 * rank, width), bf16)],
    )
    here, sent, dy_theirs = lax.optimization_barrier((here, sent, dy_theirs))
    tile_weights = lax.all_to_all(sent, ADAPTER, split_axis=0, concat_axis=0, tiled=True)

    up_ring = [(i, (i + 1) % ys) for i in range(ys)]
    down_ring = [(i, (i - 1) % ys) for i in range(ys)]
    below = lax.ppermute(here, "y", up_ring)
    above = lax.ppermute(here, "y", down_ring)
    far = jnp.stack(
        [lax.ppermute(below[0], "y", up_ring), lax.ppermute(above[1], "y", down_ring)]
    )

    tile_weights, _, _ = lax.optimization_barrier((tile_weights, below, above))
    low_part = call(
        low_kernel,
        jax.ShapeDtypeStruct((tok_rows, 2 * rank), bf16),
        [tokens, dy, tile_weights],
        [owner_of],
        8 * tok_rows * width * rank,
        3 * 2**20,
    )
    share = tok_rows // peers
    low_terms = lax.all_to_all(
        low_part.reshape(peers, share, 2 * rank), TENSOR, split_axis=0, concat_axis=0, tiled=True
    )
    far, low_terms = lax.optimization_barrier((far, low_terms))
    mine = [here, below, above, far]
    weights = mine + [lax.ppermute(w, "c", swap) for w in mine]
    steps = [0, ys - 1, 1, 2]
    at = jnp.stack(
        [xh]
        + [2 * ((y + s) % ys) + c for s in steps]
        + [2 * ((y + s) % ys) + 1 - c for s in steps]
    ).astype(jnp.int32)

    big = 2 * tok_rows * planes * width * width
    parts = call(
        back_kernel,
        jax.ShapeDtypeStruct((planes, tok_rows, width), bf16),
        [dy, dy_theirs, *weights],
        [at],
        2 * big,
        13 * 2**20,
    )
    parts, low_terms = lax.optimization_barrier((parts, low_terms))
    input_sum = lax.psum_scatter(parts, "z", scatter_dimension=0)

    low_share = jnp.sum(low_terms.astype(f32), axis=0).astype(bf16)
    low = lax.all_to_all(
        jnp.broadcast_to(low_share[None], (peers, share, 2 * rank)),
        TENSOR,
        split_axis=0,
        concat_axis=0,
        tiled=True,
    ).reshape(tok_rows, 2 * rank)
    grads_sent, lora_out, lora_grad = call(
        grad_kernel,
        (
            jax.ShapeDtypeStruct((owners, 2 * rank, width), bf16),
            jax.ShapeDtypeStruct((tok_rows, width), bf16),
            jax.ShapeDtypeStruct((tok_rows, width), bf16),
        ),
        [low, tokens, dy, tile_weights],
        [owner_of],
        16 * tok_rows * width * rank,
        6 * 2**20,
    )
    grad_parts = lax.all_to_all(grads_sent, ADAPTER, split_axis=0, concat_axis=0, tiled=True)

    x_all, grads_sent_done = lax.optimization_barrier((x_all, lora_out))
    lora_out = grads_sent_done

    out_theirs = call(
        functools.partial(forward_kernel, theirs=True),
        jax.ShapeDtypeStruct((tok_rows, width), bf16),
        [x_all, *weights],
        [at],
        big,
        8 * 2**20,
    )
    out_swapped = lax.ppermute(out_theirs, "xh", swap)
    out_mine = call(
        functools.partial(forward_kernel, theirs=False),
        jax.ShapeDtypeStruct((tok_rows, width), f32),
        [x_all, *weights],
        [at],
        big,
        8 * 2**20,
    )

    lanes = 128
    state = (
        adapter_down_weight,
        adapter_up_weight,
        down_first_moment,
        down_second_moment,
        up_first_moment,
        up_second_moment,
    )
    state_spec = pl.BlockSpec((held, rank, lanes), lambda i: (0, 0, i))
    fresh = pl.pallas_call(
        adam_kernel,
        grid=(width // lanes,),
        out_shape=[jax.ShapeDtypeStruct(adapter_down_weight.shape, f32)] * 6,
        in_specs=[SMEM, pl.BlockSpec((owners, 2 * rank, lanes), lambda i: (0, 0, i))]
        + [state_spec] * 6,
        out_specs=[state_spec] * 6,
        scratch_shapes=[pltpu.VMEM((held, 2 * rank, lanes), f32)],
        compiler_params=pltpu.CompilerParams(vmem_limit_bytes=60 * 2**20),
        cost_estimate=pl.CostEstimate(
            flops=60 * held * rank * width, bytes_accessed=8 * 2**20, transcendentals=0
        ),
    )(slots, grad_parts, *state)

    output = (out_mine + out_swapped.astype(f32) + lora_out.astype(f32)).astype(bf16)
    token_gradient = (input_sum.astype(f32) + lora_grad.astype(f32)).astype(bf16)
    return (output, token_gradient, *fresh)


def solution(mesh):
    split = Mesh(mesh.devices.reshape(2, 4, 2, 2, 8), ("xl", "y", "c", "xh", "z"))
    matrix = P(ADAPTER, TENSOR)
    table = P(ADAPTER, None)
    state = P(ADAPTER, None, TENSOR)
    return jax.shard_map(
        per_device,
        mesh=split,
        in_specs=(matrix,) * 3 + (table,) * 2 + (state,) * 6,
        out_specs=(matrix,) * 2 + (state,) * 6,
        check_vma=False,
    )
```

```python
import functools

import jax
import jax.numpy as jnp
from jax import lax
from jax.experimental import pallas as pl
from jax.experimental.pallas import tpu as pltpu
from jax.sharding import Mesh
from jax.sharding import PartitionSpec as P

ADAM_STEP = 10

adapter_scale = 0.5
beta_one = 0.9
beta_two = 0.999
adam_eps = 1e-08
weight_decay = 0.01
learn_rate = 0.001

VMEM = pl.BlockSpec(memory_space=pltpu.VMEM)
SMEM = pl.BlockSpec(memory_space=pltpu.SMEM)
ADAPTER = ("xl", "y", "c")
TENSOR = ("xh", "z")
NT = (((1,), (1,)), ((), ()))
TN = (((0,), (0,)), ((), ()))
NN = (((1,), (0,)), ((), ()))


def dot(a, b, dims):
    return lax.dot_general(a, b, dims, preferred_element_type=jnp.float32)


def call(kernel, out_shape, args, scalars, flops, moved, limit=40, scratch=()):
    return pl.pallas_call(
        kernel,
        out_shape=out_shape,
        in_specs=[SMEM] * len(scalars) + [VMEM] * len(args),
        out_specs=jax.tree.map(lambda _: VMEM, out_shape),
        scratch_shapes=list(scratch),
        compiler_params=pltpu.CompilerParams(vmem_limit_bytes=limit * 2**20),
        cost_estimate=pl.CostEstimate(flops=flops, bytes_accessed=moved, transcendentals=0),
    )(*scalars, *args)


def decoupled_adam(parameter, moment, second, gradient):
    moment_new = beta_one * moment + (1.0 - beta_one) * gradient
    second_new = beta_two * second + (1.0 - beta_two) * gradient * gradient
    bias_first = 1.0 - beta_one**ADAM_STEP
    bias_second = 1.0 - beta_two**ADAM_STEP
    update = (
        moment_new / bias_first / (jnp.sqrt(second_new / bias_second) + adam_eps)
        + weight_decay * parameter
    )
    return (parameter - learn_rate * update, moment_new, second_new)


def select_kernel(slot_ref, mine_ref, theirs_ref, send_ref):
    held = mine_ref.shape[0]

    @pl.loop(0, send_ref.shape[0] // 2)
    def _(peer):
        for side, table in enumerate((mine_ref, theirs_ref)):
            at = 2 * peer + side
            send_ref[at] = table[jnp.clip(slot_ref[at], 0, held - 1)]


def low_kernel(owner_ref, x_ref, dy_ref, weight_ref, low_ref):
    tiles = owner_ref.shape[0]
    height = x_ref.shape[0] // tiles
    rank = weight_ref.shape[1] // 2
    for j in range(tiles):
        rows = pl.ds(j * height, height)
        weight = weight_ref[owner_ref[j]]
        fwd = dot(x_ref[rows], weight, NT)
        bwd = dot(dy_ref[rows], weight, NT)
        lane = lax.broadcasted_iota(jnp.int32, fwd.shape, 1)
        low_ref[rows] = jnp.where(lane < rank, fwd, bwd).astype(jnp.bfloat16)


def grad_kernel(owner_ref, low_ref, x_ref, dy_ref, weight_ref, send_ref, out_ref, back_ref):
    tiles = owner_ref.shape[0]
    height = x_ref.shape[0] // tiles
    rank = weight_ref.shape[1] // 2
    send_ref[...] = jnp.zeros_like(send_ref)
    for j in range(tiles):
        rows = pl.ds(j * height, height)
        owner = owner_ref[j]
        weight = weight_ref[owner]
        low = low_ref[rows]
        fwd, bwd = low[:, :rank], low[:, rank:]
        out_ref[rows] = (adapter_scale * dot(fwd, weight[rank:], NN)).astype(jnp.bfloat16)
        back_ref[rows] = (adapter_scale * dot(bwd, weight[:rank], NN)).astype(jnp.bfloat16)
        up_part = dot(low, dy_ref[rows], TN)[:rank]
        down_part = dot(low, x_ref[rows], TN)[rank:]
        part = jnp.concatenate([down_part, up_part], axis=0)
        send_ref[owner] = (adapter_scale * part).astype(jnp.bfloat16)


def collect_kernel(slot_ref, part_ref, mine_ref, theirs_ref, acc):
    held = mine_ref.shape[0]
    acc[...] = jnp.zeros_like(acc)

    @pl.loop(0, part_ref.shape[0] // 2)
    def _(peer):
        for side in range(2):
            at = 2 * peer + side
            slot = slot_ref[at]

            @pl.when((slot >= 0) & (slot < held))
            def _(at=at, side=side, slot=slot):
                acc[side, slot] += part_ref[at].astype(jnp.float32)

    mine_ref[...] = acc[0]
    theirs_ref[...] = acc[1].astype(jnp.bfloat16)


def adam_kernel(mine, theirs, pd, pu, md, vd, mu, vu, npd, npu, nmd, nvd, nmu, nvu):
    held, rank, _ = pd.shape
    for k in range(held):
        grad = mine[k] + theirs[k].astype(jnp.float32)
        npd[k], nmd[k], nvd[k] = decoupled_adam(pd[k], md[k], vd[k], grad[:rank])
        npu[k], nmu[k], nvu[k] = decoupled_adam(pu[k], mu[k], vu[k], grad[rank:])


def back_kernel(at_ref, *refs):
    gradients, weights, out_ref = refs[:4], refs[4:-1], refs[-1]
    for i, weight in enumerate(weights):
        for row in range(2):
            total = dot(gradients[2 * row][...], weight[0], NT)
            total += dot(gradients[2 * row + 1][...], weight[1], NT)
            out_ref[at_ref[i], row] = total.astype(jnp.bfloat16)


def forward_kernel(at_ref, x_ref, *refs, row):
    weights, out_ref = refs[:-2], refs[-2:]
    for j, out in enumerate(out_ref):
        total = dot(x_ref[at_ref[0], row], weights[0][j], NN)
        for i, weight in enumerate(weights[1:], 1):
            total += dot(x_ref[at_ref[i], row], weight[j], NN)
        out[...] = total.astype(out.dtype)


def per_device(
    tokens,
    cotangent,
    frozen_weight,
    adapter_per_tile,
    tile_token_length,
    adapter_down_weight,
    adapter_up_weight,
    down_first_moment,
    down_second_moment,
    up_first_moment,
    up_second_moment,
):
    bf16, f32 = jnp.bfloat16, jnp.float32
    tok_rows, width = tokens.shape
    tile_count = adapter_per_tile.shape[1]
    tile_rows = tok_rows // tile_count
    held, rank, _ = adapter_down_weight.shape
    owners = lax.axis_size(ADAPTER)
    planes = lax.axis_size("z")
    ys = lax.axis_size("y")
    xl, y, c, xh = (lax.axis_index(n) for n in ("xl", "y", "c", "xh"))

    swap = [(0, 1), (1, 0)]
    plane = ("y", "c")
    adapters_mine = jnp.concatenate([adapter_down_weight, adapter_up_weight], axis=1).astype(bf16)
    adapters_theirs = lax.ppermute(adapters_mine, "xl", swap)
    adapters_here = adapter_per_tile[0]
    owner = adapters_here // held
    sites = owners // 2
    owner_of = owner % sites * 2 + (owner // sites != xl).astype(jnp.int32)
    chosen = owner_of[None, :] == jnp.arange(owners, dtype=jnp.int32)[:, None]
    asked = jnp.sum(jnp.where(chosen, adapters_here[None, :] % held - held, 0), axis=1) + held
    slots = lax.all_to_all(
        asked.reshape(sites, 2, 1), plane, split_axis=0, concat_axis=0, tiled=True
    ).reshape(owners)

    cross = [(i, 3 - i) for i in range(4)]
    half = width // 2
    own_half = lax.dynamic_slice_in_dim(tokens, xl * half, half, 1)
    other_half = lax.dynamic_slice_in_dim(tokens, (1 - xl) * half, half, 1)
    got_half = lax.ppermute(other_half, "xl", swap)

    got_half, adapters_theirs, slots = lax.optimization_barrier(
        (got_half, adapters_theirs, slots)
    )
    x_all = lax.all_gather(jnp.stack([own_half, got_half]), "z", axis=0)

    place = [0, 2, 1, 3]
    later, lengths, _ = lax.optimization_barrier((xh, tile_token_length[0], slots))
    keep = lax.dynamic_slice_in_dim(frozen_weight, later * half, half, 0)
    give = lax.dynamic_slice_in_dim(frozen_weight, (1 - later) * half, half, 0)
    first = lax.ppermute(
        give,
        ("xl", "xh"),
        [(place[0], place[1]), (place[1], place[3]), (place[3], place[2]), (place[2], place[0])],
    )
    second = lax.ppermute(keep, ("xl", "xh"), [(place[1], place[2]), (place[2], place[1])])
    position = jnp.arange(tile_rows, dtype=jnp.int32)
    kept = position[None, :] < lengths[:, None]
    dy = jnp.where(
        kept[:, :, None],
        cotangent.reshape(tile_count, tile_rows, width),
        jnp.zeros((), bf16),
    ).reshape(tok_rows, width)

    dy_x = lax.ppermute(dy, "xl", swap)
    dy_h = lax.ppermute(dy, "xh", swap)
    dy_d = lax.ppermute(dy, ("xl", "xh"), cross)

    sent = call(
        select_kernel,
        jax.ShapeDtypeStruct((owners, 2 * rank, width), bf16),
        [adapters_mine, adapters_theirs],
        [slots],
        0,
        3 * 2**20,
    )

    def exchange(blocks):
        moved = lax.all_to_all(
            blocks.reshape(sites, 4 * rank, width), plane, split_axis=0, concat_axis=0, tiled=True
        )
        return moved.reshape(owners, 2 * rank, width)

    tile_weights = exchange(sent)
    side, _ = lax.optimization_barrier((xl, tile_weights[0, 0, :1]))
    left = side == 0
    other = jnp.where(xl == xh, keep, second)
    here = jnp.stack([jnp.where(left, other, first), jnp.where(left, first, other)])

    up_ring = [(i, (i + 1) % ys) for i in range(ys)]
    down_ring = [(i, (i - 1) % ys) for i in range(ys)]
    below = lax.ppermute(here, "y", up_ring)
    above = lax.ppermute(here, "y", down_ring)
    low_part = call(
        low_kernel,
        jax.ShapeDtypeStruct((tok_rows, 2 * rank), bf16),
        [tokens, dy, tile_weights],
        [owner_of],
        8 * tok_rows * width * rank,
        3 * 2**20,
    )

    peers = lax.axis_size(TENSOR)
    share = tok_rows // peers

    def trade(blocks):
        return lax.all_to_all(blocks, TENSOR, split_axis=0, concat_axis=0, tiled=True)

    terms = trade(low_part.reshape(peers, share, 2 * rank))
    below, above, terms = lax.optimization_barrier((below, above, terms))
    far = jnp.stack(
        [lax.ppermute(below[0], "y", up_ring), lax.ppermute(above[1], "y", down_ring)]
    )
    low_share = jnp.sum(terms.astype(f32), axis=0).astype(bf16)
    low = trade(jnp.broadcast_to(low_share[None], (peers, share, 2 * rank)))
    low = low.reshape(tok_rows, 2 * rank)
    far, low = lax.optimization_barrier((far, low))
    mine = [here, below, above, far]
    weights = mine + [lax.ppermute(w, "c", swap) for w in mine]
    steps = [0, ys - 1, 1, 2]
    at = jnp.stack(
        [2 * ((y + s) % ys) + c for s in steps] + [2 * ((y + s) % ys) + 1 - c for s in steps]
    ).astype(jnp.int32)

    big = 2 * tok_rows * planes * width * half
    same = xh == 0
    gradients = [
        jnp.where(same, dy, dy_h),
        jnp.where(same, dy_h, dy),
        jnp.where(same, dy_x, dy_d),
        jnp.where(same, dy_d, dy_x),
    ]
    parts = call(
        back_kernel,
        jax.ShapeDtypeStruct((planes, 2, tok_rows, half), bf16),
        [*gradients, *weights],
        [at],
        4 * big,
        13 * 2**20,
    )
    sums = lax.psum_scatter(parts, "z", scatter_dimension=0)
    sum_own, sum_got = sums[0], sums[1]
    sum_back = lax.ppermute(sum_got, "xl", swap)
    input_sum = jnp.concatenate(
        [jnp.where(left, sum_own, sum_back), jnp.where(left, sum_back, sum_own)], axis=1
    )

    grads_sent, lora_out, lora_grad = call(
        grad_kernel,
        (
            jax.ShapeDtypeStruct((owners, 2 * rank, width), bf16),
            jax.ShapeDtypeStruct((tok_rows, width), bf16),
            jax.ShapeDtypeStruct((tok_rows, width), bf16),
        ),
        [low, tokens, dy, tile_weights],
        [owner_of],
        16 * tok_rows * width * rank,
        6 * 2**20,
    )

    x_all, grads_sent, lora_out = lax.optimization_barrier((x_all, grads_sent, lora_out))
    grad_parts = exchange(grads_sent)
    block = jax.ShapeDtypeStruct((tok_rows, width), bf16)
    forward = [
        call(
            functools.partial(forward_kernel, row=row),
            (block, block),
            [x_all, *weights],
            [at],
            2 * big,
            8 * 2**20,
        )
        for row in (1, 0)
    ]
    (got_a, got_b), (own_a, own_b) = forward
    from_x = lax.ppermute(jnp.where(same, got_a, got_b), "xl", swap)
    from_d = lax.ppermute(jnp.where(same, got_b, got_a), ("xl", "xh"), cross)
    from_h = lax.ppermute(jnp.where(same, own_b, own_a), "xh", swap)
    out_mine = jnp.where(same, own_a, own_b).astype(f32)
    out_mine += from_x.astype(f32) + from_d.astype(f32) + from_h.astype(f32)

    lanes = 128
    state = (
        adapter_down_weight,
        adapter_up_weight,
        down_first_moment,
        down_second_moment,
        up_first_moment,
        up_second_moment,
    )
    state_spec = pl.BlockSpec((held, rank, lanes), lambda i: (0, 0, i))
    grad_spec = pl.BlockSpec((held, 2 * rank, lanes), lambda i: (0, 0, i))
    grad_shape = (held, 2 * rank, width)
    grad_mine, grad_theirs = pl.pallas_call(
        collect_kernel,
        grid=(width // lanes,),
        out_shape=[
            jax.ShapeDtypeStruct(grad_shape, f32),
            jax.ShapeDtypeStruct(grad_shape, bf16),
        ],
        in_specs=[SMEM, pl.BlockSpec((owners, 2 * rank, lanes), lambda i: (0, 0, i))],
        out_specs=[grad_spec] * 2,
        scratch_shapes=[pltpu.VMEM((2, held, 2 * rank, lanes), f32)],
        compiler_params=pltpu.CompilerParams(vmem_limit_bytes=24 * 2**20),
        cost_estimate=pl.CostEstimate(
            flops=2 * owners * rank * width, bytes_accessed=4 * 2**20, transcendentals=0
        ),
    )(slots, grad_parts)
    fresh = pl.pallas_call(
        adam_kernel,
        grid=(width // lanes,),
        out_shape=[jax.ShapeDtypeStruct(adapter_down_weight.shape, f32)] * 6,
        in_specs=[grad_spec] * 2 + [state_spec] * 6,
        out_specs=[state_spec] * 6,
        compiler_params=pltpu.CompilerParams(vmem_limit_bytes=60 * 2**20),
        cost_estimate=pl.CostEstimate(
            flops=60 * held * rank * width, bytes_accessed=8 * 2**20, transcendentals=0
        ),
    )(grad_mine, lax.ppermute(grad_theirs, "xl", swap), *state)

    output = (out_mine + lora_out.astype(f32)).astype(bf16)
    token_gradient = (input_sum.astype(f32) + lora_grad.astype(f32)).astype(bf16)
    return (output, token_gradient, *fresh)


def solution(mesh):
    split = Mesh(mesh.devices.reshape(2, 4, 2, 2, 8), ("xl", "y", "c", "xh", "z"))
    matrix = P(ADAPTER, TENSOR)
    table = P(ADAPTER, None)
    state = P(ADAPTER, None, TENSOR)
    return jax.shard_map(
        per_device,
        mesh=split,
        in_specs=(matrix,) * 3 + (table,) * 2 + (state,) * 6,
        out_specs=(matrix,) * 2 + (state,) * 6,
        check_vma=False,
    )
```

```python
import functools

import jax
import jax.numpy as jnp
from jax import lax
from jax.experimental import pallas as pl
from jax.experimental.pallas import tpu as pltpu
from jax.sharding import Mesh
from jax.sharding import PartitionSpec as P

ADAM_STEP = 10

adapter_scale = 0.5
beta_one = 0.9
beta_two = 0.999
adam_eps = 1e-08
weight_decay = 0.01
learn_rate = 0.001

VMEM = pl.BlockSpec(memory_space=pltpu.VMEM)
SMEM = pl.BlockSpec(memory_space=pltpu.SMEM)
ADAPTER = ("xl", "y", "c")
TENSOR = ("xh", "z")
NT = (((1,), (1,)), ((), ()))
TN = (((0,), (0,)), ((), ()))
NN = (((1,), (0,)), ((), ()))


def dot(a, b, dims):
    return lax.dot_general(a, b, dims, preferred_element_type=jnp.float32)


def call(kernel, out_shape, args, scalars, flops, moved, limit=40, scratch=()):
    return pl.pallas_call(
        kernel,
        out_shape=out_shape,
        in_specs=[SMEM] * len(scalars) + [VMEM] * len(args),
        out_specs=jax.tree.map(lambda _: VMEM, out_shape),
        scratch_shapes=list(scratch),
        compiler_params=pltpu.CompilerParams(vmem_limit_bytes=limit * 2**20),
        cost_estimate=pl.CostEstimate(flops=flops, bytes_accessed=moved, transcendentals=0),
    )(*scalars, *args)


def decoupled_adam(parameter, moment, second, gradient):
    moment_new = beta_one * moment + (1.0 - beta_one) * gradient
    second_new = beta_two * second + (1.0 - beta_two) * gradient * gradient
    bias_first = 1.0 - beta_one**ADAM_STEP
    bias_second = 1.0 - beta_two**ADAM_STEP
    update = (
        moment_new / bias_first / (jnp.sqrt(second_new / bias_second) + adam_eps)
        + weight_decay * parameter
    )
    return (parameter - learn_rate * update, moment_new, second_new)


def select_kernel(slot_ref, mine_ref, theirs_ref, send_ref):
    held = mine_ref.shape[0]

    @pl.loop(0, send_ref.shape[0] // 2)
    def _(peer):
        for side, table in enumerate((mine_ref, theirs_ref)):
            at = 2 * peer + side
            send_ref[at] = table[jnp.clip(slot_ref[at], 0, held - 1)]


def low_kernel(owner_ref, x_ref, dy_ref, weight_ref, low_ref):
    tiles = owner_ref.shape[0]
    height = x_ref.shape[0] // tiles
    rank = weight_ref.shape[1] // 2
    for j in range(tiles):
        rows = pl.ds(j * height, height)
        weight = weight_ref[owner_ref[j]]
        fwd = dot(x_ref[rows], weight, NT)
        bwd = dot(dy_ref[rows], weight, NT)
        lane = lax.broadcasted_iota(jnp.int32, fwd.shape, 1)
        low_ref[rows] = jnp.where(lane < rank, fwd, bwd).astype(jnp.bfloat16)


def grad_kernel(owner_ref, low_ref, x_ref, dy_ref, weight_ref, send_ref, out_ref, back_ref):
    tiles = owner_ref.shape[0]
    height = x_ref.shape[0] // tiles
    rank = weight_ref.shape[1] // 2
    send_ref[...] = jnp.zeros_like(send_ref)
    for j in range(tiles):
        rows = pl.ds(j * height, height)
        owner = owner_ref[j]
        weight = weight_ref[owner]
        low = low_ref[rows]
        fwd, bwd = low[:, :rank], low[:, rank:]
        out_ref[rows] = (adapter_scale * dot(fwd, weight[rank:], NN)).astype(jnp.bfloat16)
        back_ref[rows] = (adapter_scale * dot(bwd, weight[:rank], NN)).astype(jnp.bfloat16)
        up_part = dot(low, dy_ref[rows], TN)[:rank]
        down_part = dot(low, x_ref[rows], TN)[rank:]
        part = jnp.concatenate([down_part, up_part], axis=0)
        send_ref[owner] = (adapter_scale * part).astype(jnp.bfloat16)


def collect(slot_ref, part_ref, acc, side):
    held = acc.shape[0]
    acc[...] = jnp.zeros_like(acc)

    @pl.loop(0, part_ref.shape[0] // 2)
    def _(peer):
        at = 2 * peer + side
        slot = slot_ref[at]

        @pl.when((slot >= 0) & (slot < held))
        def _():
            acc[slot] += part_ref[at].astype(jnp.float32)


def collect_kernel(slot_ref, part_ref, theirs_ref, acc):
    collect(slot_ref, part_ref, acc, 1)
    theirs_ref[...] = acc[...].astype(jnp.bfloat16)


def adam_kernel(
    slot_ref, part_ref, theirs, pd, pu, md, vd, mu, vu, npd, npu, nmd, nvd, nmu, nvu, acc
):
    held, rank, _ = pd.shape
    collect(slot_ref, part_ref, acc, 0)
    for k in range(held):
        grad = acc[k] + theirs[k].astype(jnp.float32)
        npd[k], nmd[k], nvd[k] = decoupled_adam(pd[k], md[k], vd[k], grad[:rank])
        npu[k], nmu[k], nvu[k] = decoupled_adam(pu[k], mu[k], vu[k], grad[rank:])


def back_kernel(at_ref, *refs):
    gradients, weights, out_ref = refs[:4], refs[4:-1], refs[-1]
    column = at_ref[len(weights)]
    for i, weight in enumerate(weights):
        for row in range(2):
            total = dot(gradients[2 * row][...], weight[column], NT)
            total += dot(gradients[2 * row + 1][...], weight[1 - column], NT)
            out_ref[at_ref[i], row] = total.astype(jnp.bfloat16)


def forward_kernel(at_ref, x_ref, *refs, row):
    weights, out_ref = refs[:-2], refs[-2:]
    for j, out in enumerate(out_ref):
        total = dot(x_ref[at_ref[0], row], weights[0][j], NN)
        for i, weight in enumerate(weights[1:], 1):
            total += dot(x_ref[at_ref[i], row], weight[j], NN)
        out[...] = total.astype(out.dtype)


def per_device(
    tokens,
    cotangent,
    frozen_weight,
    adapter_per_tile,
    tile_token_length,
    adapter_down_weight,
    adapter_up_weight,
    down_first_moment,
    down_second_moment,
    up_first_moment,
    up_second_moment,
):
    bf16, f32 = jnp.bfloat16, jnp.float32
    tok_rows, width = tokens.shape
    tile_count = adapter_per_tile.shape[1]
    tile_rows = tok_rows // tile_count
    held, rank, _ = adapter_down_weight.shape
    owners = lax.axis_size(ADAPTER)
    planes = lax.axis_size("z")
    ys = lax.axis_size("y")
    xl, y, c, xh = (lax.axis_index(n) for n in ("xl", "y", "c", "xh"))

    swap = [(0, 1), (1, 0)]
    plane = ("y", "c")
    adapters_mine = jnp.concatenate([adapter_down_weight, adapter_up_weight], axis=1).astype(bf16)
    adapters_theirs = lax.ppermute(adapters_mine, "xl", swap)
    adapters_here = adapter_per_tile[0]
    owner = adapters_here // held
    sites = owners // 2
    owner_of = owner % sites * 2 + (owner // sites != xl).astype(jnp.int32)
    chosen = owner_of[None, :] == jnp.arange(owners, dtype=jnp.int32)[:, None]
    asked = jnp.sum(jnp.where(chosen, adapters_here[None, :] % held - held, 0), axis=1) + held
    slots = lax.all_to_all(
        asked.reshape(sites, 2, 1), plane, split_axis=0, concat_axis=0, tiled=True
    ).reshape(owners)

    cross = [(i, 3 - i) for i in range(4)]
    half = width // 2
    own_half = lax.dynamic_slice_in_dim(tokens, xl * half, half, 1)
    other_half = lax.dynamic_slice_in_dim(tokens, (1 - xl) * half, half, 1)
    got_half = lax.ppermute(other_half, "xl", swap)

    got_half, adapters_theirs, slots = lax.optimization_barrier(
        (got_half, adapters_theirs, slots)
    )
    x_all = lax.all_gather(jnp.stack([own_half, got_half]), "z", axis=0)

    place = [0, 2, 1, 3]
    later, lengths, _ = lax.optimization_barrier((xh, tile_token_length[0], slots))
    keep = lax.dynamic_slice_in_dim(frozen_weight, later * half, half, 0)
    give = lax.dynamic_slice_in_dim(frozen_weight, (1 - later) * half, half, 0)
    first = lax.ppermute(
        give,
        ("xl", "xh"),
        [(place[0], place[1]), (place[1], place[3]), (place[3], place[2]), (place[2], place[0])],
    )
    second = lax.ppermute(keep, ("xl", "xh"), [(place[1], place[2]), (place[2], place[1])])
    position = jnp.arange(tile_rows, dtype=jnp.int32)
    kept = position[None, :] < lengths[:, None]
    dy = jnp.where(
        kept[:, :, None],
        cotangent.reshape(tile_count, tile_rows, width),
        jnp.zeros((), bf16),
    ).reshape(tok_rows, width)

    dy_x = lax.ppermute(dy, "xl", swap)
    dy_h = lax.ppermute(dy, "xh", swap)
    dy_d = lax.ppermute(dy, ("xl", "xh"), cross)

    sent = call(
        select_kernel,
        jax.ShapeDtypeStruct((owners, 2 * rank, width), bf16),
        [adapters_mine, adapters_theirs],
        [slots],
        0,
        3 * 2**20,
    )

    def exchange(blocks):
        moved = lax.all_to_all(
            blocks.reshape(sites, 4 * rank, width), plane, split_axis=0, concat_axis=0, tiled=True
        )
        return moved.reshape(owners, 2 * rank, width)

    tile_weights = exchange(sent)
    side, _ = lax.optimization_barrier((xl, tile_weights[0, 0, :1]))
    left = side == 0
    other = jnp.where(xl == xh, keep, second)
    here = jnp.stack([jnp.where(left, other, first), jnp.where(left, first, other)])

    up_ring = [(i, (i + 1) % ys) for i in range(ys)]
    down_ring = [(i, (i - 1) % ys) for i in range(ys)]
    below = lax.ppermute(here, "y", up_ring)
    above = lax.ppermute(here, "y", down_ring)
    far = lax.ppermute(here, "y", [(i, (i + 2) % ys) for i in range(ys)])
    low_part = call(
        low_kernel,
        jax.ShapeDtypeStruct((tok_rows, 2 * rank), bf16),
        [tokens, dy, tile_weights],
        [owner_of],
        8 * tok_rows * width * rank,
        3 * 2**20,
    )

    peers = lax.axis_size(TENSOR)
    share = tok_rows // peers

    def trade(blocks):
        return lax.all_to_all(blocks, TENSOR, split_axis=0, concat_axis=0, tiled=True)

    terms = trade(low_part.reshape(peers, share, 2 * rank))
    here, below, above, _ = lax.optimization_barrier((here, below, above, low_part))
    far, _ = lax.optimization_barrier((far, terms))
    mine = [here, below, above, far]
    weights = mine + [lax.ppermute(w, "c", swap) for w in mine]
    steps = [0, ys - 1, 1, 2]
    at = jnp.stack(
        [2 * ((y + s) % ys) + c for s in steps]
        + [2 * ((y + s) % ys) + 1 - c for s in steps]
        + [xh]
    ).astype(jnp.int32)

    low_share = jnp.sum(terms.astype(f32), axis=0).astype(bf16)
    low = trade(jnp.broadcast_to(low_share[None], (peers, share, 2 * rank)))
    low = low.reshape(tok_rows, 2 * rank)
    at, low = lax.optimization_barrier((at, low))
    big = 2 * tok_rows * planes * width * half
    same = xh == 0
    parts = call(
        back_kernel,
        jax.ShapeDtypeStruct((planes, 2, tok_rows, half), bf16),
        [dy, dy_h, dy_x, dy_d, *weights],
        [at],
        4 * big,
        13 * 2**20,
    )
    sums = lax.psum_scatter(parts, "z", scatter_dimension=0)
    sum_own, sum_got = sums[0], sums[1]
    sum_back = lax.ppermute(sum_got, "xl", swap)
    input_sum = jnp.concatenate(
        [jnp.where(left, sum_own, sum_back), jnp.where(left, sum_back, sum_own)], axis=1
    )

    grads_sent, lora_out, lora_grad = call(
        grad_kernel,
        (
            jax.ShapeDtypeStruct((owners, 2 * rank, width), bf16),
            jax.ShapeDtypeStruct((tok_rows, width), bf16),
            jax.ShapeDtypeStruct((tok_rows, width), bf16),
        ),
        [low, tokens, dy, tile_weights],
        [owner_of],
        16 * tok_rows * width * rank,
        6 * 2**20,
        limit=58,
    )

    x_all, grads_sent, lora_out = lax.optimization_barrier((x_all, grads_sent, lora_out))
    grad_parts = exchange(grads_sent)
    block = jax.ShapeDtypeStruct((tok_rows, width), bf16)
    forward = [
        call(
            functools.partial(forward_kernel, row=row),
            (block, block),
            [x_all, *weights],
            [at],
            2 * big,
            8 * 2**20,
        )
        for row in (1, 0)
    ]
    (got_a, got_b), (own_a, own_b) = forward
    from_x = lax.ppermute(jnp.where(same, got_a, got_b), "xl", swap)
    from_d = lax.ppermute(jnp.where(same, got_b, got_a), ("xl", "xh"), cross)
    from_h = lax.ppermute(jnp.where(same, own_b, own_a), "xh", swap)
    out_mine = jnp.where(same, own_a, own_b).astype(f32)
    out_mine += from_x.astype(f32) + from_d.astype(f32) + from_h.astype(f32)

    lanes = 128
    state = (
        adapter_down_weight,
        adapter_up_weight,
        down_first_moment,
        down_second_moment,
        up_first_moment,
        up_second_moment,
    )
    state_spec = pl.BlockSpec((held, rank, lanes), lambda i: (0, 0, i))
    grad_spec = pl.BlockSpec((held, 2 * rank, lanes), lambda i: (0, 0, i))
    grad_shape = (held, 2 * rank, width)
    part_spec = pl.BlockSpec((owners, 2 * rank, lanes), lambda i: (0, 0, i))
    acc = pltpu.VMEM((held, 2 * rank, lanes), f32)
    grad_theirs = pl.pallas_call(
        collect_kernel,
        grid=(width // lanes,),
        out_shape=jax.ShapeDtypeStruct(grad_shape, bf16),
        in_specs=[SMEM, part_spec],
        out_specs=grad_spec,
        scratch_shapes=[acc],
        compiler_params=pltpu.CompilerParams(vmem_limit_bytes=24 * 2**20),
        cost_estimate=pl.CostEstimate(
            flops=owners * rank * width, bytes_accessed=3 * 2**20, transcendentals=0
        ),
    )(slots, grad_parts)
    fresh = pl.pallas_call(
        adam_kernel,
        grid=(width // lanes,),
        out_shape=[jax.ShapeDtypeStruct(adapter_down_weight.shape, f32)] * 6,
        in_specs=[SMEM, part_spec, grad_spec] + [state_spec] * 6,
        out_specs=[state_spec] * 6,
        scratch_shapes=[acc],
        compiler_params=pltpu.CompilerParams(vmem_limit_bytes=60 * 2**20),
        cost_estimate=pl.CostEstimate(
            flops=60 * held * rank * width, bytes_accessed=8 * 2**20, transcendentals=0
        ),
    )(slots, grad_parts, lax.ppermute(grad_theirs, "xl", swap), *state)

    output = (out_mine + lora_out.astype(f32)).astype(bf16)
    token_gradient = (input_sum.astype(f32) + lora_grad.astype(f32)).astype(bf16)
    return (output, token_gradient, *fresh)


def solution(mesh):
    split = Mesh(mesh.devices.reshape(2, 4, 2, 2, 8), ("xl", "y", "c", "xh", "z"))
    matrix = P(ADAPTER, TENSOR)
    table = P(ADAPTER, None)
    state = P(ADAPTER, None, TENSOR)
    return jax.shard_map(
        per_device,
        mesh=split,
        in_specs=(matrix,) * 3 + (table,) * 2 + (state,) * 6,
        out_specs=(matrix,) * 2 + (state,) * 6,
        check_vma=False,
    )
```

```python
import functools

import jax
import jax.numpy as jnp
from jax import lax
from jax.experimental import pallas as pl
from jax.experimental.pallas import tpu as pltpu
from jax.sharding import Mesh
from jax.sharding import PartitionSpec as P

ADAM_STEP = 10

adapter_scale = 0.5
beta_one = 0.9
beta_two = 0.999
adam_eps = 1e-08
weight_decay = 0.01
learn_rate = 0.001

VMEM = pl.BlockSpec(memory_space=pltpu.VMEM)
SMEM = pl.BlockSpec(memory_space=pltpu.SMEM)
ADAPTER = ("xl", "y", "c")
TENSOR = ("xh", "z")
NT = (((1,), (1,)), ((), ()))
TN = (((0,), (0,)), ((), ()))
NN = (((1,), (0,)), ((), ()))


def dot(a, b, dims):
    return lax.dot_general(a, b, dims, preferred_element_type=jnp.float32)


def call(kernel, out_shape, args, scalars, flops, moved, limit=40, scratch=()):
    return pl.pallas_call(
        kernel,
        out_shape=out_shape,
        in_specs=[SMEM] * len(scalars) + [VMEM] * len(args),
        out_specs=jax.tree.map(lambda _: VMEM, out_shape),
        scratch_shapes=list(scratch),
        compiler_params=pltpu.CompilerParams(vmem_limit_bytes=limit * 2**20),
        cost_estimate=pl.CostEstimate(flops=flops, bytes_accessed=moved, transcendentals=0),
    )(*scalars, *args)


def decoupled_adam(parameter, moment, second, gradient):
    moment_new = beta_one * moment + (1.0 - beta_one) * gradient
    second_new = beta_two * second + (1.0 - beta_two) * gradient * gradient
    bias_first = 1.0 - beta_one**ADAM_STEP
    bias_second = 1.0 - beta_two**ADAM_STEP
    update = (
        moment_new / bias_first / (jnp.sqrt(second_new / bias_second) + adam_eps)
        + weight_decay * parameter
    )
    return (parameter - learn_rate * update, moment_new, second_new)


def select_kernel(slot_ref, mine_ref, theirs_ref, send_ref):
    held = mine_ref.shape[0]

    @pl.loop(0, send_ref.shape[0] // 2)
    def _(peer):
        for side, table in enumerate((mine_ref, theirs_ref)):
            at = 2 * peer + side
            send_ref[at] = table[jnp.clip(slot_ref[at], 0, held - 1)]


def low_kernel(owner_ref, x_ref, dy_ref, weight_ref, low_ref):
    tiles = owner_ref.shape[0]
    height = x_ref.shape[0] // tiles
    rank = weight_ref.shape[1] // 2
    for j in range(tiles):
        rows = pl.ds(j * height, height)
        weight = weight_ref[owner_ref[j]]
        fwd = dot(x_ref[rows], weight, NT)
        bwd = dot(dy_ref[rows], weight, NT)
        lane = lax.broadcasted_iota(jnp.int32, fwd.shape, 1)
        low_ref[rows] = jnp.where(lane < rank, fwd, bwd).astype(jnp.bfloat16)


def grad_kernel(owner_ref, low_ref, x_ref, dy_ref, weight_ref, send_ref, out_ref, back_ref):
    tiles = owner_ref.shape[0]
    height = x_ref.shape[0] // tiles
    rank = weight_ref.shape[1] // 2
    send_ref[...] = jnp.zeros_like(send_ref)
    for j in range(tiles):
        rows = pl.ds(j * height, height)
        owner = owner_ref[j]
        weight = weight_ref[owner]
        low = low_ref[rows]
        fwd, bwd = low[:, :rank], low[:, rank:]
        out_ref[rows] = (adapter_scale * dot(fwd, weight[rank:], NN)).astype(jnp.bfloat16)
        back_ref[rows] = (adapter_scale * dot(bwd, weight[:rank], NN)).astype(jnp.bfloat16)
        up_part = dot(low, dy_ref[rows], TN)[:rank]
        down_part = dot(low, x_ref[rows], TN)[rank:]
        part = jnp.concatenate([down_part, up_part], axis=0)
        send_ref[owner] = (adapter_scale * part).astype(jnp.bfloat16)


def collect(slot_ref, part_ref, acc, side):
    held = acc.shape[0]
    acc[...] = jnp.zeros_like(acc)

    @pl.loop(0, part_ref.shape[0] // 2)
    def _(peer):
        at = 2 * peer + side
        slot = slot_ref[at]

        @pl.when((slot >= 0) & (slot < held))
        def _():
            acc[slot] += part_ref[at].astype(jnp.float32)


def collect_kernel(slot_ref, part_ref, theirs_ref, acc):
    collect(slot_ref, part_ref, acc, 1)
    theirs_ref[...] = acc[...].astype(jnp.bfloat16)


def adam_kernel(
    slot_ref, part_ref, theirs, pd, pu, md, vd, mu, vu, npd, npu, nmd, nvd, nmu, nvu, acc
):
    held, rank, _ = pd.shape
    collect(slot_ref, part_ref, acc, 0)
    for k in range(held):
        grad = acc[k] + theirs[k].astype(jnp.float32)
        npd[k], nmd[k], nvd[k] = decoupled_adam(pd[k], md[k], vd[k], grad[:rank])
        npu[k], nmu[k], nvu[k] = decoupled_adam(pu[k], mu[k], vu[k], grad[rank:])


def back_kernel(at_ref, *refs):
    gradients, weights, out_ref = refs[:4], refs[4:-1], refs[-1]
    column = at_ref[len(weights)]
    for i, weight in enumerate(weights):
        for row in range(2):
            total = dot(gradients[2 * row][...], weight[column], NT)
            total += dot(gradients[2 * row + 1][...], weight[1 - column], NT)
            out_ref[at_ref[i], row] = total.astype(jnp.bfloat16)


def forward_kernel(at_ref, x_ref, *refs, row):
    weights, out_ref = refs[:-2], refs[-2:]
    for j, out in enumerate(out_ref):
        total = dot(x_ref[at_ref[0], row], weights[0][j], NN)
        for i, weight in enumerate(weights[1:], 1):
            total += dot(x_ref[at_ref[i], row], weight[j], NN)
        out[...] = total.astype(out.dtype)


def per_device(
    tokens,
    cotangent,
    frozen_weight,
    adapter_per_tile,
    tile_token_length,
    adapter_down_weight,
    adapter_up_weight,
    down_first_moment,
    down_second_moment,
    up_first_moment,
    up_second_moment,
):
    bf16, f32 = jnp.bfloat16, jnp.float32
    tok_rows, width = tokens.shape
    tile_count = adapter_per_tile.shape[1]
    tile_rows = tok_rows // tile_count
    held, rank, _ = adapter_down_weight.shape
    owners = lax.axis_size(ADAPTER)
    planes = lax.axis_size("z")
    ys = lax.axis_size("y")
    xl, y, c, xh = (lax.axis_index(n) for n in ("xl", "y", "c", "xh"))

    swap = [(0, 1), (1, 0)]
    plane = ("y", "c")
    adapters_mine = jnp.concatenate([adapter_down_weight, adapter_up_weight], axis=1).astype(bf16)
    adapters_theirs = lax.ppermute(adapters_mine, "xl", swap)
    adapters_here = adapter_per_tile[0]
    owner = adapters_here // held
    sites = owners // 2
    owner_of = owner % sites * 2 + (owner // sites != xl).astype(jnp.int32)
    chosen = owner_of[None, :] == jnp.arange(owners, dtype=jnp.int32)[:, None]
    asked = jnp.sum(jnp.where(chosen, adapters_here[None, :] % held - held, 0), axis=1) + held
    slots = lax.all_to_all(
        asked.reshape(sites, 2, 1), plane, split_axis=0, concat_axis=0, tiled=True
    ).reshape(owners)

    cross = [(i, 3 - i) for i in range(4)]
    half = width // 2
    own_half = lax.dynamic_slice_in_dim(tokens, xl * half, half, 1)
    other_half = lax.dynamic_slice_in_dim(tokens, (1 - xl) * half, half, 1)
    got_half = lax.ppermute(other_half, "xl", swap)

    got_half, adapters_theirs, slots = lax.optimization_barrier(
        (got_half, adapters_theirs, slots)
    )
    x_all = lax.all_gather(jnp.stack([own_half, got_half]), "z", axis=0)

    place = [0, 2, 1, 3]
    later, lengths, _ = lax.optimization_barrier((xh, tile_token_length[0], slots))
    keep = lax.dynamic_slice_in_dim(frozen_weight, later * half, half, 0)
    give = lax.dynamic_slice_in_dim(frozen_weight, (1 - later) * half, half, 0)
    first = lax.ppermute(
        give,
        ("xl", "xh"),
        [(place[0], place[1]), (place[1], place[3]), (place[3], place[2]), (place[2], place[0])],
    )
    second = lax.ppermute(keep, ("xl", "xh"), [(place[1], place[2]), (place[2], place[1])])
    position = jnp.arange(tile_rows, dtype=jnp.int32)
    kept = position[None, :] < lengths[:, None]
    dy = jnp.where(
        kept[:, :, None],
        cotangent.reshape(tile_count, tile_rows, width),
        jnp.zeros((), bf16),
    ).reshape(tok_rows, width)

    dy_x = lax.ppermute(dy, "xl", swap)
    dy_h = lax.ppermute(dy, "xh", swap)
    dy_d = lax.ppermute(dy, ("xl", "xh"), cross)

    sent = call(
        select_kernel,
        jax.ShapeDtypeStruct((owners, 2 * rank, width), bf16),
        [adapters_mine, adapters_theirs],
        [slots],
        0,
        3 * 2**20,
    )

    def exchange(blocks):
        moved = lax.all_to_all(
            blocks.reshape(sites, 4 * rank, width), plane, split_axis=0, concat_axis=0, tiled=True
        )
        return moved.reshape(owners, 2 * rank, width)

    tile_weights = exchange(sent)
    side, _ = lax.optimization_barrier((xl, tile_weights[0, 0, :1]))
    left = side == 0
    other = jnp.where(xl == xh, keep, second)
    here = jnp.stack([jnp.where(left, other, first), jnp.where(left, first, other)])

    up_ring = [(i, (i + 1) % ys) for i in range(ys)]
    down_ring = [(i, (i - 1) % ys) for i in range(ys)]
    below = lax.ppermute(here, "y", up_ring)
    above = lax.ppermute(here, "y", down_ring)
    far = lax.ppermute(here, "y", [(i, (i + 2) % ys) for i in range(ys)])
    low_part = call(
        low_kernel,
        jax.ShapeDtypeStruct((tok_rows, 2 * rank), bf16),
        [tokens, dy, tile_weights],
        [owner_of],
        8 * tok_rows * width * rank,
        3 * 2**20,
    )

    peers = lax.axis_size(TENSOR)
    share = tok_rows // peers

    def trade(blocks):
        return lax.all_to_all(blocks, TENSOR, split_axis=0, concat_axis=0, tiled=True)

    terms = trade(low_part.reshape(peers, share, 2 * rank))
    here, below, above, _ = lax.optimization_barrier((here, below, above, low_part))
    far, _ = lax.optimization_barrier((far, terms))
    mine = [here, below, above, far]
    weights = mine + [lax.ppermute(w, "c", swap) for w in mine]
    steps = [0, ys - 1, 1, 2]
    at = jnp.stack(
        [2 * ((y + s) % ys) + c for s in steps]
        + [2 * ((y + s) % ys) + 1 - c for s in steps]
        + [xh]
    ).astype(jnp.int32)

    low_share = jnp.sum(terms.astype(f32), axis=0).astype(bf16)
    low = trade(jnp.broadcast_to(low_share[None], (peers, share, 2 * rank)))
    low = low.reshape(tok_rows, 2 * rank)
    big = 2 * tok_rows * planes * width * half
    same = xh == 0
    parts = call(
        back_kernel,
        jax.ShapeDtypeStruct((planes, 2, tok_rows, half), bf16),
        [dy, dy_h, dy_x, dy_d, *weights],
        [at],
        4 * big,
        13 * 2**20,
    )
    parts, low = lax.optimization_barrier((parts, low))
    sums = lax.psum_scatter(parts, "z", scatter_dimension=0)
    sum_own, sum_got = sums[0], sums[1]
    sum_back = lax.ppermute(sum_got, "xl", swap)
    input_sum = jnp.concatenate(
        [jnp.where(left, sum_own, sum_back), jnp.where(left, sum_back, sum_own)], axis=1
    )

    grads_sent, lora_out, lora_grad = call(
        grad_kernel,
        (
            jax.ShapeDtypeStruct((owners, 2 * rank, width), bf16),
            jax.ShapeDtypeStruct((tok_rows, width), bf16),
            jax.ShapeDtypeStruct((tok_rows, width), bf16),
        ),
        [low, tokens, dy, tile_weights],
        [owner_of],
        16 * tok_rows * width * rank,
        6 * 2**20,
        limit=58,
    )

    x_all, grads_sent, lora_out = lax.optimization_barrier((x_all, grads_sent, lora_out))
    grad_parts = exchange(grads_sent)
    block = jax.ShapeDtypeStruct((tok_rows, width), bf16)
    def forward(row, at):
        return call(
            functools.partial(forward_kernel, row=row),
            (block, block),
            [x_all, *weights],
            [at],
            2 * big,
            8 * 2**20,
        )

    got_a, got_b = forward(1, at)
    at, got_a, got_b = lax.optimization_barrier((at, got_a, got_b))
    own_a, own_b = forward(0, at)
    from_x = lax.ppermute(jnp.where(same, got_a, got_b), "xl", swap)
    from_d = lax.ppermute(jnp.where(same, got_b, got_a), ("xl", "xh"), cross)
    from_h = lax.ppermute(jnp.where(same, own_b, own_a), "xh", swap)
    out_mine = jnp.where(same, own_a, own_b).astype(f32)
    out_mine += from_x.astype(f32) + from_d.astype(f32) + from_h.astype(f32)

    lanes = 128
    state = (
        adapter_down_weight,
        adapter_up_weight,
        down_first_moment,
        down_second_moment,
        up_first_moment,
        up_second_moment,
    )
    state_spec = pl.BlockSpec((held, rank, lanes), lambda i: (0, 0, i))
    grad_spec = pl.BlockSpec((held, 2 * rank, lanes), lambda i: (0, 0, i))
    grad_shape = (held, 2 * rank, width)
    part_spec = pl.BlockSpec((owners, 2 * rank, lanes), lambda i: (0, 0, i))
    acc = pltpu.VMEM((held, 2 * rank, lanes), f32)
    grad_theirs = pl.pallas_call(
        collect_kernel,
        grid=(width // lanes,),
        out_shape=jax.ShapeDtypeStruct(grad_shape, bf16),
        in_specs=[SMEM, part_spec],
        out_specs=grad_spec,
        scratch_shapes=[acc],
        compiler_params=pltpu.CompilerParams(vmem_limit_bytes=24 * 2**20),
        cost_estimate=pl.CostEstimate(
            flops=owners * rank * width, bytes_accessed=3 * 2**20, transcendentals=0
        ),
    )(slots, grad_parts)
    fresh = pl.pallas_call(
        adam_kernel,
        grid=(width // lanes,),
        out_shape=[jax.ShapeDtypeStruct(adapter_down_weight.shape, f32)] * 6,
        in_specs=[SMEM, part_spec, grad_spec] + [state_spec] * 6,
        out_specs=[state_spec] * 6,
        scratch_shapes=[acc],
        compiler_params=pltpu.CompilerParams(vmem_limit_bytes=60 * 2**20),
        cost_estimate=pl.CostEstimate(
            flops=60 * held * rank * width, bytes_accessed=8 * 2**20, transcendentals=0
        ),
    )(slots, grad_parts, lax.ppermute(grad_theirs, "xl", swap), *state)

    output = (out_mine + lora_out.astype(f32)).astype(bf16)
    token_gradient = (input_sum.astype(f32) + lora_grad.astype(f32)).astype(bf16)
    return (output, token_gradient, *fresh)


def solution(mesh):
    split = Mesh(mesh.devices.reshape(2, 4, 2, 2, 8), ("xl", "y", "c", "xh", "z"))
    matrix = P(ADAPTER, TENSOR)
    table = P(ADAPTER, None)
    state = P(ADAPTER, None, TENSOR)
    return jax.shard_map(
        per_device,
        mesh=split,
        in_specs=(matrix,) * 3 + (table,) * 2 + (state,) * 6,
        out_specs=(matrix,) * 2 + (state,) * 6,
        check_vma=False,
    )
```
